128 devices in a mesh: db: 16 (over y, x), seq: 8 (over z, core).
Axes of the slice: x: 4, y: 4, z: 4, core: 2. Of those that a mesh axis runs over, the one named last changes fastest.
Arguments:
- self_query: bfloat16 [49152, 2048], P(('db', 'seq')), may hold values from -500 to 500
- self_key: bfloat16 [49152, 2048], P(('db', 'seq')), may hold values from -6 to 6
- self_value: bfloat16 [49152, 2048], P(('db', 'seq')), may hold values from -6 to 6
- cross_query: bfloat16 [49152, 2048], P(('db', 'seq')), may hold values from -700 to 700
- retrieval_shard: int32 [768, 2], P(('db', 'seq')), may hold values from 0 to 15, all different within a row; in each aligned block of 6 rows (0 to 5, 6 to 11, ...) at most 2 rows name the same one
- retrieval_row: int32 [768, 2], P(('db', 'seq')), may hold values from 0 to 31
- database: bfloat16 [512, 64, 896], P('db'), may hold values from -6 to 6
- ffn_in: bfloat16 [896, 3584], P(None, 'db'), may hold values from -0.1875 to 0.1875
- ffn_out: bfloat16 [3584, 896], P('db'), may hold values from -0.09375 to 0.09375
- cross_projection: bfloat16 [896, 4096], P(None, 'db'), may hold values from -0.1875 to 0.1875
Outputs:
- self_attended: bfloat16 [49152, 2048], P(('db', 'seq'))
- cross_attended: bfloat16 [49152, 2048], P(('db', 'seq'))
The draws below stay inside these ranges and needn't reach their ends.
Inputs may be any that keep to these rules, and one draw needn't show every extreme that they name: `retrieval_shard`: each row names 2 different shards; among the rows of one device no shard is named more than 2 times, a bound that some block reaches.
All inputs are finite; a program needn't handle non-finite values.
Results may differ from the reference program's by a relative error of at most 0.04.
Values may be sent and summed in bfloat16 or wider, within the bound.
No kernel may reach another device: no remote copies, remote signals or barrier semaphores. Data moves between devices by JAX's collectives and lax.ppermute only.
A program may use at most 256 MiB of HBM per device.

```python
import math
from functools import partial
import jax
import jax.numpy as jnp
import numpy as np
from jax import lax

HEADS = 16
HEAD_DIM = 128
E = 896
FFE = 3584
STRETCH = 64
NEIGH = 2
NTOK = 64
CAP = 2
DB_ROWS = 32
TOKENS = 49152
STRETCHES = 768
CH_DEV = 6
DB_TOTAL = 512
N_DB = 16


def drawn_pair(key):
    shape = (TOKENS, HEADS * HEAD_DIM)
    queries = jax.random.truncated_normal(jax.random.fold_in(key, 21), -5.0, 5.0, shape, jnp.float32)
    keys = jax.random.truncated_normal(jax.random.fold_in(key, 22), -5.0, 5.0, shape, jnp.float32)
    return (queries, keys)


def draw_self_query(key, part):
    queries, keys = drawn_pair(key)
    return queries.astype(jnp.bfloat16)


def draw_self_key(key, part):
    queries, keys = drawn_pair(key)
    return keys.astype(jnp.bfloat16)


def draw_cross_query(key, part):
    key = jax.random.fold_in(key, 5)
    values = jax.random.truncated_normal(key, -5.0, 5.0, (TOKENS, HEADS * HEAD_DIM), jnp.float32)
    return values.astype(jnp.bfloat16)


def touch_ends(values, key, least, largest):
    dims = values.shape
    index_at = [jax.random.randint(jax.random.fold_in(key, axis), (), 0, dims[axis]) for axis in range(len(dims))]
    values = values.at[tuple(index_at)].set(least)
    longest = dims.index(max(dims))
    index_at[longest] = (index_at[longest] + 1) % dims[longest]
    return values.at[tuple(index_at)].set(largest)


def shard_levels(key, extent, cuts, least, high):
    def one(position, shards_of):
        heights = jax.random.uniform(jax.random.fold_in(jax.random.fold_in(key, 6), position), (shards_of,), jnp.float32, least / len(cuts), high / len(cuts))
        return jnp.repeat(jnp.exp(heights), extent[position] // shards_of).reshape((-1,) + (1,) * (len(extent) - position - 1))

    gain = one(*cuts[0])
    for cut in cuts[1:]:
        gain = gain * one(*cut)
    return gain


def routed_block(own_key, own, number, rows, amount, top, reach, lean):
    sequence = jax.random.permutation(own_key, amount)
    heavy_load, ordinary = load_shares(amount, rows * top, reach, lean, True), load_shares(amount, rows * top, reach, lean, False)
    places = jnp.arange(amount)

    def named(lengths, offset_by):
        used = int((lengths > 0).sum())
        fixed = max(1, used // 4)
        moved = fixed + (places - fixed + offset_by * (used - fixed)) % max(1, amount - fixed)
        return jnp.zeros((amount,), jnp.int32).at[sequence[jnp.where(places < fixed, places, moved)]].set(jnp.asarray(lengths, jnp.int32))

    lengths = jnp.where(number % 4 == 0, named(heavy_load, number // 4), named(ordinary, number - number // 4 - 1))
    mixed = jax.random.permutation(jax.random.fold_in(own, 3), amount)
    giver, taker = mixed[0:amount // 2 * 2:2], mixed[1:amount // 2 * 2:2]
    room = jnp.minimum(lengths[giver] - 1, reach - lengths[taker]) // 2
    room = jnp.where((giver == sequence[0]) | (taker == sequence[0]) | (lengths[taker] == 0), 0, jnp.maximum(room, 0))
    moved = jax.random.randint(jax.random.fold_in(own, 4), (amount // 2,), 0, 1 << 20) % (room + 1)
    lengths = lengths.at[giver].add(-moved).at[taker].add(moved)
    items = jnp.searchsorted(jnp.cumsum(lengths), jnp.arange(rows * top), side="right").astype(jnp.int32)
    table = items.reshape(top, rows).T
    table = table[jax.random.permutation(jax.random.fold_in(own, 1), rows)]
    offset_by = jax.random.randint(jax.random.fold_in(own, 2), (rows, 1), 0, top)
    return jnp.take_along_axis(table, (jnp.arange(top)[None, :] + offset_by) % top, axis=1)


def load_shares(number_of, total, most, lean, full):
    loads = [(1 << 20) // math.isqrt(grade ** lean) + 1 for grade in range(1, number_of + 1)]
    largest = most if full else min(most, max(-(-total // number_of), total * loads[0] // sum(loads)))
    least = 1 if total - largest >= number_of - 1 else 0
    given, spare = [largest] + [least] * (number_of - 1), total - largest - least * (number_of - 1)
    while spare > 0:
        free = [i for i in range(1, number_of) if given[i] < largest] or [i for i in range(1, number_of) if given[i] < most]
        pool, budget = sum([loads[i] for i in free]), spare
        for i in free:
            more = min(most - given[i], max(1, budget * loads[i] // pool), spare)
            given[i] = given[i] + more
            spare = spare - more
    return np.array(given)


def scatter_about(key, extent, scale, bound, shards=(), kind=jnp.bfloat16):
    entries = jax.random.normal(key, extent, jnp.float32) * scale
    if len(shards) > 0:
        entries = shard_levels(key, extent, shards, -0.22, 0.18) * entries
    return jnp.clip(entries, min=-bound, max=bound).astype(kind)


def setup_inputs(seed: int = 0) -> dict:
    seeds = jax.random.split(jax.random.key(seed), 11)
    self_query = draw_self_query(jax.random.fold_in(seeds[10], 71), 0)
    self_key = draw_self_key(jax.random.fold_in(seeds[10], 71), 0)
    self_value = scatter_about(seeds[2], (TOKENS, HEADS * HEAD_DIM), 1.0, 6.0, ((0, 128),))
    cross_query = draw_cross_query(jax.random.fold_in(seeds[10], 71), 0)
    retrieval_shard_keys = jax.random.split(jax.random.fold_in(seeds[4], 1), STRETCHES // CH_DEV)
    retrieval_shard_turns = jax.random.permutation(jax.random.fold_in(seeds[4], 3), STRETCHES // CH_DEV)
    retrieval_shard = jax.vmap(lambda own, number: routed_block(jax.random.fold_in(seeds[4], 2), own, number, CH_DEV, N_DB, NEIGH, CAP, 2))(retrieval_shard_keys, retrieval_shard_turns).reshape((STRETCHES, NEIGH))
    retrieval_row = touch_ends(jax.random.randint(seeds[5], (STRETCHES, NEIGH), 0, DB_ROWS), jax.random.fold_in(seeds[5], 1), 0, DB_ROWS - 1).astype(jnp.int32)
    database = scatter_about(seeds[6], (DB_TOTAL, NTOK, E), 1.0, 6.0, ((0, 16),))
    ffn_in = scatter_about(seeds[7], (E, FFE), E ** -0.5, 0.1875, ((1, 16),))
    ffn_out = scatter_about(seeds[8], (FFE, E), FFE ** -0.5, 0.09375, ((0, 16),))
    cross_projection = scatter_about(seeds[9], (E, 2 * HEADS * HEAD_DIM), E ** -0.5, 0.1875, ((1, 16),))
    return {"self_query": self_query, "self_key": self_key, "self_value": self_value, "cross_query": cross_query, "retrieval_shard": retrieval_shard, "retrieval_row": retrieval_row, "database": database, "ffn_in": ffn_in, "ffn_out": ffn_out, "cross_projection": cross_projection}


HIGH = lax.Precision.HIGHEST

def normalize(values):
    wide = values.astype(jnp.float32)
    return (wide * lax.rsqrt(lax.optimization_barrier(jnp.mean(wide * wide, axis=-1, keepdims=True)) + 1e-06)).astype(jnp.bfloat16)

def sequence_layer(pieces, database, ffn_in, ffn_out, cross_projection):
    self_query, self_key, self_value, cross_query, shard_ids, row_ids = pieces
    length = self_query.shape[0]
    width = HEADS * HEAD_DIM
    scale = 1.0 / math.sqrt(HEAD_DIM)
    wanted = (shard_ids * DB_ROWS + row_ids).reshape(-1).astype(jnp.int32)
    found = jnp.take(database, wanted, axis=0)
    neighbours = found.reshape(-1, found.shape[-1])
    normed_in = normalize(neighbours)
    expanded = jax.nn.gelu(jnp.dot(normed_in, ffn_in, preferred_element_type=jnp.float32), approximate=True).astype(jnp.bfloat16)
    encoded = (neighbours.astype(jnp.float32) + jnp.dot(expanded, ffn_out, preferred_element_type=jnp.float32)).astype(jnp.bfloat16)
    projected = jnp.dot(normalize(encoded), cross_projection, preferred_element_type=jnp.float32).astype(jnp.bfloat16)
    count = length // STRETCH
    span = NEIGH * NTOK
    projected = projected.reshape(count, span, 2, HEADS, HEAD_DIM).astype(jnp.float32)
    projected = jnp.concatenate([jnp.zeros((1, span, 2, HEADS, HEAD_DIM), jnp.float32), projected], axis=0)
    padded = jnp.concatenate([jnp.zeros((1, width), jnp.float32), cross_query.astype(jnp.float32), jnp.zeros((STRETCH - 1, width), jnp.float32)], axis=0)
    grouped = padded.reshape(count + 1, STRETCH, HEADS, HEAD_DIM)
    scores = jnp.einsum('gqhd,gkhd->ghqk', grouped, projected[:, :, 0], precision=HIGH) * scale
    probs = jnp.exp(scores - lax.optimization_barrier(jnp.max(scores, axis=-1, keepdims=True)))
    weights = lax.optimization_barrier(probs.astype(jnp.bfloat16)).astype(jnp.float32)
    cross_out = jnp.einsum('ghqk,gkhd->gqhd', weights, projected[:, :, 1], precision=HIGH)
    cross_out = cross_out / jnp.transpose(lax.optimization_barrier(jnp.sum(probs, axis=-1)), (0, 2, 1))[..., None]
    cross_attended = cross_out.reshape(-1, width)[1:length + 1].astype(jnp.bfloat16)
    query = self_query.astype(jnp.float32).reshape(length, HEADS, HEAD_DIM)
    keys = self_key.astype(jnp.float32).reshape(length, HEADS, HEAD_DIM)
    values = self_value.astype(jnp.float32).reshape(length, HEADS, HEAD_DIM)
    scores = jnp.einsum('qhd,khd->hqk', query, keys, precision=HIGH) * scale
    allowed = jnp.arange(length)[None, :] <= jnp.arange(length)[:, None]
    scores = jnp.where(allowed[None], scores, -1e+30)
    probs = jnp.where(allowed[None], jnp.exp(scores - lax.optimization_barrier(jnp.max(scores, axis=-1, keepdims=True))), 0.0)
    weights = lax.optimization_barrier(probs.astype(jnp.bfloat16)).astype(jnp.float32)
    self_out = jnp.einsum('hqk,khd->qhd', weights, values, precision=HIGH)
    self_out = self_out / jnp.transpose(lax.optimization_barrier(jnp.sum(probs, axis=-1)))[:, :, None]
    return (self_out.reshape(length, width).astype(jnp.bfloat16), cross_attended)

def by_sequence(array):
    return array.reshape((N_DB, array.shape[0] // N_DB) + array.shape[1:])

def reference(self_query, self_key, self_value, cross_query, retrieval_shard, retrieval_row, database, ffn_in, ffn_out, cross_projection):
    pieces = (by_sequence(self_query), by_sequence(self_key), by_sequence(self_value), by_sequence(cross_query), by_sequence(retrieval_shard), by_sequence(retrieval_row))
    layer = partial(sequence_layer, database=database, ffn_in=ffn_in, ffn_out=ffn_out, cross_projection=cross_projection)
    self_all, cross_all = lax.map(layer, pieces)
    width = HEADS * HEAD_DIM
    return (self_all.reshape(-1, width), cross_all.reshape(-1, width))
```

```python
import functools
import math

import jax
import jax.numpy as jnp
from jax import lax
from jax.experimental import pallas as pl
from jax.experimental.pallas import tpu as pltpu
from jax.sharding import PartitionSpec as P

HEADS = 16
HEAD_DIM = 128
STRETCH = 64
NEIGH = 2
CAP = 2
LOG2E = 1.4426950408889634
BF16 = jnp.bfloat16
F32 = jnp.float32
NT = (((1,), (1,)), ((), ()))
ANY = pl.BlockSpec(memory_space=pl.ANY)
VMEM = pl.BlockSpec(memory_space=pltpu.VMEM)
HOPS = ((0, 0), (2, 0), (2, 1), (1, 0), (3, 0), (1, 1), (3, 1), (0, 1))


def cost(flops, size, exps=0):
    return pl.CostEstimate(flops=int(flops), bytes_accessed=int(size), transcendentals=int(exps))


def params(mib=56, **more):
    return pltpu.CompilerParams(vmem_limit_bytes=mib << 20, **more)


def hop(value, chips, flip):
    count = lax.axis_size("seq")
    pairs = [(i, ((i + 2 * chips) % count) ^ flip) for i in range(count)]
    return lax.ppermute(value, "seq", pairs)


def run_copies(copies):
    for copy in copies:
        copy.start()
    for copy in copies:
        copy.wait()


def rms(wide):
    return wide * lax.rsqrt(jnp.mean(wide * wide, axis=-1, keepdims=True) + 1e-06)


def fetch_kernel(asked, database, found, sem):
    run_copies(
        [
            pltpu.make_async_copy(database.at[asked[i]], found.at[i], sem.at[i])
            for i in range(found.shape[0])
        ]
    )


def fetch(asked, database):
    slots = asked.shape[0]
    shape = (slots, *database.shape[1:])
    return pl.pallas_call(
        fetch_kernel,
        grid_spec=pltpu.PrefetchScalarGridSpec(
            num_scalar_prefetch=1,
            grid=(1,),
            in_specs=[ANY],
            out_specs=ANY,
            scratch_shapes=[pltpu.SemaphoreType.DMA((slots,))],
        ),
        out_shape=jax.ShapeDtypeStruct(shape, BF16),
        cost_estimate=cost(0, 4 * math.prod(shape)),
        compiler_params=params(),
        name="fetch",
    )(asked, database)


def ffn_blocks(xn, gathered, half):
    count = gathered.shape[0]
    w_in = jnp.concatenate([gathered[b, :half] for b in range(count)], axis=0)
    w_out = jnp.concatenate([gathered[b, half:] for b in range(count)], axis=0)
    hidden = lax.dot_general(xn, w_in, NT, preferred_element_type=F32)
    hidden = jax.nn.gelu(hidden, approximate=True).astype(BF16)
    return jnp.dot(hidden, w_out, preferred_element_type=F32)


def ffn_first_kernel(half, slot, arrived, gathered, total, normed, x, sem):
    tokens = arrived.shape[1]

    @pl.when(pl.program_id(0) == 0)
    def _():
        run_copies(
            [
                pltpu.make_async_copy(
                    arrived.at[slot[i]], x.at[i * tokens : (i + 1) * tokens], sem.at[i]
                )
                for i in range(x.shape[0] // tokens)
            ]
        )
        wide = x[...].astype(F32)
        normed[...] = rms(wide).astype(BF16)
        total[...] = wide

    total[...] += ffn_blocks(normed[...], gathered, half)


def ffn_second_kernel(half, normed, before, gathered, out, total):
    @pl.when(pl.program_id(0) == 0)
    def _():
        total[...] = before[...]

    total[...] += ffn_blocks(normed[...], gathered, half)

    @pl.when(pl.program_id(0) == pl.num_programs(0) - 1)
    def _():
        encoded = total[...].astype(BF16).astype(F32)
        out[...] = rms(encoded).astype(BF16)


def ffn_first(slot, arrived, gathered, half):
    requests = slot.shape[0]
    rows, width = requests * arrived.shape[1], arrived.shape[2]
    owners = gathered.shape[0]
    step = 4
    whole = lambda i, s: (0, 0)
    return pl.pallas_call(
        functools.partial(ffn_first_kernel, half),
        grid_spec=pltpu.PrefetchScalarGridSpec(
            num_scalar_prefetch=1,
            grid=(owners // step,),
            in_specs=[ANY, pl.BlockSpec((step, 2 * half, width), lambda i, s: (i, 0, 0))],
            out_specs=[pl.BlockSpec((rows, width), whole), pl.BlockSpec((rows, width), whole)],
            scratch_shapes=[pltpu.VMEM((rows, width), BF16), pltpu.SemaphoreType.DMA((requests,))],
        ),
        out_shape=[
            jax.ShapeDtypeStruct((rows, width), F32),
            jax.ShapeDtypeStruct((rows, width), BF16),
        ],
        cost_estimate=cost(4 * rows * width * owners * half, 16e6, rows * owners * half),
        compiler_params=params(),
        name="ffn_first",
    )(slot, arrived, gathered)


def ffn_second(normed, before, gathered, half):
    rows, width = normed.shape
    owners = gathered.shape[0]
    step = 4
    whole = pl.BlockSpec((rows, width), lambda i: (0, 0))
    return pl.pallas_call(
        functools.partial(ffn_second_kernel, half),
        grid=(owners // step,),
        in_specs=[whole, whole, pl.BlockSpec((step, 2 * half, width), lambda i: (i, 0, 0))],
        out_specs=whole,
        out_shape=jax.ShapeDtypeStruct((rows, width), BF16),
        scratch_shapes=[pltpu.VMEM((rows, width), F32)],
        cost_estimate=cost(4 * rows * width * owners * half, 16e6, rows * owners * half),
        compiler_params=params(),
        name="ffn_second",
    )(normed, before, gathered)


def attend(query, keys, values, allowed, scale):
    scores = lax.dot_general(query, keys, NT, preferred_element_type=F32)
    if allowed is not None:
        scores = jnp.where(allowed, scores, -jnp.inf)
    probs = jnp.exp2((scores - jnp.max(scores, axis=-1, keepdims=True)) * scale)
    total = jnp.sum(probs, axis=-1, keepdims=True)
    return jnp.dot(probs.astype(BF16), values, preferred_element_type=F32) / total


def cross_kernel(first, scale, core, normed, mine, other, query, ahead, out, sent, weights, sem):
    step = pl.program_id(0)
    groups = weights.shape[0]
    width = weights.shape[2]
    d = HEAD_DIM
    own = pl.multiple_of(core[0] * d, d)
    rest = pl.multiple_of((1 - core[0]) * d, d)

    def copies(j):
        found = []
        for part in range(2):
            for t, (source, place) in enumerate(((mine, own), (other, rest))):
                found.append(
                    pltpu.make_async_copy(
                        source.at[part * groups + j, first:, :],
                        weights.at[j, pl.ds(part * 2 * d + place, d), :],
                        sem.at[j, 2 * part + t],
                    )
                )
        return found

    @pl.when(step == 0)
    def _():
        for j in range(groups):
            for copy in copies(j):
                copy.start()

    for copy in copies(step):
        copy.wait()
    pairs = lax.dot_general(normed[...], weights[step], NT, preferred_element_type=F32).astype(BF16)
    span = NEIGH * STRETCH
    stretches = normed.shape[0] // span
    at_row = lax.broadcasted_iota(jnp.int32, (STRETCH, 2 * span), 0)
    at_key = lax.broadcasted_iota(jnp.int32, (STRETCH, 2 * span), 1)
    allowed = (at_row == STRETCH - 1) == (at_key >= span)
    for t in range(2):
        lanes = slice(t * d, (t + 1) * d)
        keys = pairs[:, t * d : (t + 1) * d]
        values = pairs[:, (2 + t) * d : (3 + t) * d]
        for b in range(stretches):
            rows = slice(b * STRETCH, (b + 1) * STRETCH)
            low, high = max(b - 1, 0) * span, (b + 1) * span
            out[rows, lanes] = attend(
                query[rows, lanes], keys[low:high], values[low:high], allowed if b else None, scale
            ).astype(BF16)
        sent[:, lanes] = attend(
            ahead[:, lanes], keys[-span:], values[-span:], None, scale
        ).astype(BF16)


def cross(core, normed, mine, other, query, ahead, half):
    rows, width = query.shape
    first = 2 * half
    groups = mine.shape[0] // 2
    d = HEAD_DIM
    column = lambda j, c: (0, j)
    deep = normed.shape[1]
    return pl.pallas_call(
        functools.partial(cross_kernel, first, LOG2E / math.sqrt(d)),
        grid_spec=pltpu.PrefetchScalarGridSpec(
            num_scalar_prefetch=1,
            grid=(groups,),
            in_specs=[
                pl.BlockSpec(normed.shape, lambda j, c: (0, 0)),
                ANY,
                ANY,
                pl.BlockSpec((rows, 2 * d), column),
                pl.BlockSpec((STRETCH, 2 * d), column),
            ],
            out_specs=[
                pl.BlockSpec((rows, 2 * d), column),
                pl.BlockSpec((STRETCH, 2 * d), column),
            ],
            scratch_shapes=[
                pltpu.VMEM((groups, 4 * d, deep), BF16),
                pltpu.SemaphoreType.DMA((groups, 4)),
            ],
        ),
        out_shape=[
            jax.ShapeDtypeStruct(query.shape, BF16),
            jax.ShapeDtypeStruct(ahead.shape, BF16),
        ],
        cost_estimate=cost(2 * normed.shape[0] * deep * 4 * d * groups * 2, 12e6, rows * 256 * 16),
        compiler_params=params(),
        name="cross",
    )(core, normed, mine, other, query, ahead)


def place_of(chip, core, hop_of, chips):
    return lax.rem(chip + hop_of[0], chips), jnp.bitwise_xor(core, hop_of[1])


def pack_kernel(where, query, key, value, *rest):
    parts, sem = rest[:-1], rest[-1]
    block = parts[0].shape[2]
    copies = []
    for n, part in enumerate(parts):
        columns = pl.ds(pl.multiple_of(where[n] * block, block), block)
        for a, source in enumerate((query, key, value)):
            copies.append(
                pltpu.make_async_copy(source.at[:, columns], part.at[a], sem.at[n, a])
            )
    run_copies(copies)


def pack(where, query, key, value):
    rows, width = query.shape
    count = len(HOPS)
    shape = (3, rows, width // count)
    return pl.pallas_call(
        pack_kernel,
        grid_spec=pltpu.PrefetchScalarGridSpec(
            num_scalar_prefetch=1,
            grid=(1,),
            in_specs=[ANY] * 3,
            out_specs=[ANY] * count,
            scratch_shapes=[pltpu.SemaphoreType.DMA((count, 3))],
        ),
        out_shape=[jax.ShapeDtypeStruct(shape, BF16)] * count,
        cost_estimate=cost(0, 12 * rows * width),
        compiler_params=params(),
        name="pack",
    )(where, query, key, value)


def self_kernel(scale, source, *refs):
    count = len(HOPS)
    parts, outs = refs[:count], refs[count : 2 * count]
    query, key, value, result = refs[2 * count :]
    rows = parts[0].shape[1]
    d = HEAD_DIM
    for n in range(count):
        place = pl.ds(pl.multiple_of(source[n] * rows, rows), rows)
        query[place, :] = parts[n][0]
        key[place, :] = parts[n][1]
        value[place, :d] = parts[n][2]
    value[:, d:] = jnp.ones((count * rows, d), BF16)
    at_row = lax.broadcasted_iota(jnp.int32, (rows, rows), 0)
    at_key = lax.broadcasted_iota(jnp.int32, (rows, rows), 1)
    allowed = at_key <= at_row
    for i in range(count):
        low, high = i * rows, (i + 1) * rows
        block = query[low:high, :]
        scores = lax.dot_general(block, key[low:high, :], NT, preferred_element_type=F32)
        scores = jnp.where(allowed, scores, -jnp.inf)
        if i:
            left = lax.dot_general(block, key[:low, :], NT, preferred_element_type=F32)
            scores = jnp.concatenate([left, scores], axis=1)
        best = jnp.max(scores, axis=-1, keepdims=True)
        probs = jnp.exp2((scores - best) * scale).astype(BF16)
        summed = jnp.dot(probs, value[:high, :], preferred_element_type=F32)
        result[low:high, :] = (summed[:, :d] / summed[:, d:]).astype(BF16)
    for n in range(count):
        place = pl.ds(pl.multiple_of(source[n] * rows, rows), rows)
        outs[n][...] = result[place, :]


def self_attention(source, parts):
    count = len(HOPS)
    _, rows, width = parts[0].shape
    d = HEAD_DIM
    length = count * rows
    return pl.pallas_call(
        functools.partial(self_kernel, LOG2E / math.sqrt(d)),
        grid_spec=pltpu.PrefetchScalarGridSpec(
            num_scalar_prefetch=1,
            grid=(width // d,),
            in_specs=[pl.BlockSpec((3, rows, d), lambda h, s: (0, 0, h))] * count,
            out_specs=[pl.BlockSpec((rows, d), lambda h, s: (0, h))] * count,
            scratch_shapes=[
                pltpu.VMEM((length, d), BF16),
                pltpu.VMEM((length, d), BF16),
                pltpu.VMEM((length, 2 * d), BF16),
                pltpu.VMEM((length, d), BF16),
            ],
        ),
        out_shape=[jax.ShapeDtypeStruct((rows, width), BF16)] * count,
        cost_estimate=cost(3 * length * length * d * 2, 8e6, length * length),
        compiler_params=params(),
        name="causal",
    )(source, *parts)


def unpack_kernel(where, *refs):
    parts, out, sem = refs[:-2], refs[-2], refs[-1]
    block = parts[0].shape[1]
    run_copies(
        [
            pltpu.make_async_copy(
                part, out.at[:, pl.ds(pl.multiple_of(where[n] * block, block), block)], sem.at[n]
            )
            for n, part in enumerate(parts)
        ]
    )


def unpack(where, parts):
    rows, block = parts[0].shape
    count = len(parts)
    return pl.pallas_call(
        unpack_kernel,
        grid_spec=pltpu.PrefetchScalarGridSpec(
            num_scalar_prefetch=1,
            grid=(1,),
            in_specs=[ANY] * count,
            out_specs=ANY,
            scratch_shapes=[pltpu.SemaphoreType.DMA((count,))],
        ),
        out_shape=jax.ShapeDtypeStruct((rows, block * count), BF16),
        cost_estimate=cost(0, 4 * rows * block * count),
        compiler_params=params(),
        name="unpack",
    )(where, *parts)


def requests_of(retrieval_shard, retrieval_row):
    shard_list = retrieval_shard.reshape(-1)
    row_list = retrieval_row.reshape(-1)
    owners = lax.axis_size("db")
    order = jnp.arange(shard_list.shape[0])
    earlier = (order[:, None] > order[None, :]) & (shard_list[:, None] == shard_list[None, :])
    rank = jnp.sum(earlier.astype(jnp.int32), axis=1)
    slot = shard_list * CAP + rank
    hits = jnp.arange(owners * CAP)[:, None] == slot[None, :]
    wanted = jnp.sum(jnp.where(hits, row_list[None, :], 0), axis=1).reshape(owners, CAP)
    asked = lax.all_to_all(wanted, "db", split_axis=0, concat_axis=0, tiled=True)
    return slot, asked.reshape(-1)


def shards(
    self_query,
    self_key,
    self_value,
    cross_query,
    retrieval_shard,
    retrieval_row,
    database,
    ffn_in,
    ffn_out,
    cross_projection,
):
    owners = lax.axis_size("db")
    count = lax.axis_size("seq")
    chips = count // 2
    place = lax.axis_index("seq")
    chip, core = place // 2, place % 2
    half = ffn_out.shape[0] // 2
    deep = ffn_out.shape[1]
    width = self_query.shape[1]

    part = jnp.concatenate(
        [
            lax.dynamic_slice_in_dim(ffn_in.T, core * half, half, 0),
            lax.dynamic_slice_in_dim(ffn_out, core * half, half, 0),
            lax.dynamic_slice_in_dim(cross_projection.T, core * HEAD_DIM, HEAD_DIM, 0),
        ],
        axis=0,
    )
    mine = lax.all_gather(part, "db", axis=0, tiled=True).reshape(owners, -1, deep)
    other = hop(mine, 0, 1)

    slot, asked = requests_of(retrieval_shard, retrieval_row)
    asked = jnp.clip(asked, 0, database.shape[0] - 1)
    found = fetch(asked, database)
    arrived = lax.all_to_all(found, "db", split_axis=0, concat_axis=0, tiled=True)

    ahead = lax.ppermute(cross_query[:STRETCH], "seq", [(i, i - 1) for i in range(1, count)])

    target = jnp.stack([((core ^ f) * chips + (chip + k) % chips) for k, f in HOPS])
    source = jnp.stack([((chip - k) % chips * 2 + (core ^ f)) for k, f in HOPS])
    parts = pack(target.astype(jnp.int32), self_query, self_key, self_value)
    parts = [parts[0]] + [hop(p, k, f) for p, (k, f) in zip(parts[1:], HOPS[1:])]
    done = self_attention(source.astype(jnp.int32), parts)
    back = [done[0]] + [hop(p, chips - k, f) for p, (k, f) in zip(done[1:], HOPS[1:])]
    self_attended = unpack(target.astype(jnp.int32), back)

    total, normed_in = ffn_first(slot, arrived, mine, half)
    normed_out = ffn_second(normed_in, total, other, half)
    own, sent = cross(
        core.reshape(1).astype(jnp.int32), normed_out, mine, other, cross_query, ahead, half
    )
    before = lax.ppermute(sent, "seq", [(i, i + 1) for i in range(count - 1)])
    last = jnp.arange(STRETCH)[:, None] == STRETCH - 1
    head = jnp.where(last, own[:STRETCH], before)
    cross_attended = lax.dynamic_update_slice(own, head, (0, 0))
    return (self_attended, cross_attended)


def solution(mesh):
    in_specs = (
        P(("db", "seq"), None),
        P(("db", "seq"), None),
        P(("db", "seq"), None),
        P(("db", "seq"), None),
        P(("db", "seq"), None),
        P(("db", "seq"), None),
        P("db", None, None),
        P(None, "db"),
        P("db", None),
        P(None, "db"),
    )
    out_specs = (P(("db", "seq"), None), P(("db", "seq"), None))
    return jax.shard_map(shards, mesh=mesh, in_specs=in_specs, out_specs=out_specs, check_vma=False)
```

```python
import functools
import math

import jax
import jax.numpy as jnp
from jax import lax
from jax.experimental import pallas as pl
from jax.experimental.pallas import tpu as pltpu
from jax.sharding import PartitionSpec as P

HEADS = 16
HEAD_DIM = 128
STRETCH = 64
NEIGH = 2
CAP = 2
LOG2E = 1.4426950408889634
BF16 = jnp.bfloat16
F32 = jnp.float32
NT = (((1,), (1,)), ((), ()))
ANY = pl.BlockSpec(memory_space=pl.ANY)
VMEM = pl.BlockSpec(memory_space=pltpu.VMEM)
HOPS = ((0, 0), (2, 0), (2, 1), (1, 0), (3, 0), (1, 1), (3, 1), (0, 1))


def cost(flops, size, exps=0):
    return pl.CostEstimate(flops=int(flops), bytes_accessed=int(size), transcendentals=int(exps))


def params(mib=56, **more):
    return pltpu.CompilerParams(vmem_limit_bytes=mib << 20, **more)


def hop(value, chips, flip):
    count = lax.axis_size("seq")
    pairs = [(i, ((i + 2 * chips) % count) ^ flip) for i in range(count)]
    return lax.ppermute(value, "seq", pairs)


def run_copies(copies):
    for copy in copies:
        copy.start()
    for copy in copies:
        copy.wait()


def rms(wide):
    return wide * lax.rsqrt(jnp.mean(wide * wide, axis=-1, keepdims=True) + 1e-06)


def relay(reads, writes):
    for copy in reads:
        copy.start()
    for read, write in zip(reads, writes):
        read.wait()
        write.start()
    for copy in writes:
        copy.wait()


def fetch_kernel(asked, database, found, held, sem):
    last = database.shape[0] - 1
    count = found.shape[0]
    relay(
        [
            pltpu.make_async_copy(
                database.at[jnp.clip(asked[i], 0, last)], held.at[i], sem.at[0, i]
            )
            for i in range(count)
        ],
        [pltpu.make_async_copy(held.at[i], found.at[i], sem.at[1, i]) for i in range(count)],
    )


def fetch(asked, database):
    slots = asked.shape[0]
    shape = (slots, *database.shape[1:])
    return pl.pallas_call(
        fetch_kernel,
        grid_spec=pltpu.PrefetchScalarGridSpec(
            num_scalar_prefetch=1,
            grid=(1,),
            in_specs=[ANY],
            out_specs=ANY,
            scratch_shapes=[pltpu.VMEM(shape, BF16), pltpu.SemaphoreType.DMA((2, slots))],
        ),
        out_shape=jax.ShapeDtypeStruct(shape, BF16),
        cost_estimate=cost(0, 4 * math.prod(shape)),
        compiler_params=params(),
        name="fetch",
    )(asked, database)


def rows_of(gathered, target, first, sems, owner):
    size = target.shape[0] // gathered.shape[0]
    return pltpu.make_async_copy(
        gathered.at[owner, first : first + size, :],
        target.at[owner * size : (owner + 1) * size, :],
        sems.at[owner],
    )


def encode_kernel(
    first, slot, arrived, gathered, out, x, normed, w_in, w_out, hidden, x_sem, in_sem, out_sem
):
    tokens = arrived.shape[1]
    owners = gathered.shape[0]
    size = w_in.shape[0] // owners
    picks = [
        pltpu.make_async_copy(
            arrived.at[slot[i]], x.at[i * tokens : (i + 1) * tokens, :], x_sem.at[i]
        )
        for i in range(x.shape[0] // tokens)
    ]
    ins = [rows_of(gathered, w_in, first, in_sem, b) for b in range(owners)]
    outs = [rows_of(gathered, w_out, first + size, out_sem, b) for b in range(owners)]
    for copy in picks + ins + outs:
        copy.start()
    for copy in picks + ins + outs:
        copy.wait()
    normed[...] = rms(x[...].astype(F32)).astype(BF16)
    step = 512
    blocks = w_in.shape[0] // step

    def expand(j):
        rows = w_in[j * step : (j + 1) * step, :]
        return lax.dot_general(normed[...], rows, NT, preferred_element_type=F32)

    now = expand(0)
    for j in range(blocks):
        later = expand(j + 1) if j + 1 < blocks else None
        hidden[:, j * step : (j + 1) * step] = jax.nn.gelu(now, approximate=True).astype(BF16)
        now = later
    mixed = jnp.dot(hidden[...], w_out[...], preferred_element_type=F32)
    encoded = (x[...].astype(F32) + mixed).astype(BF16).astype(F32)
    out[...] = rms(encoded).astype(BF16)


def encode(slot, arrived, gathered, first, size):
    requests = slot.shape[0]
    rows, deep = requests * arrived.shape[1], arrived.shape[2]
    owners = gathered.shape[0]
    return pl.pallas_call(
        functools.partial(encode_kernel, first),
        grid_spec=pltpu.PrefetchScalarGridSpec(
            num_scalar_prefetch=1,
            grid=(1,),
            in_specs=[ANY, ANY],
            out_specs=pl.BlockSpec((rows, deep), lambda i, s: (0, 0)),
            scratch_shapes=[
                pltpu.VMEM((rows, deep), BF16),
                pltpu.VMEM((rows, deep), BF16),
                pltpu.VMEM((owners * size, deep), BF16),
                pltpu.VMEM((owners * size, deep), BF16),
                pltpu.VMEM((rows, owners * size), BF16),
                pltpu.SemaphoreType.DMA((requests,)),
                pltpu.SemaphoreType.DMA((owners,)),
                pltpu.SemaphoreType.DMA((owners,)),
            ],
        ),
        out_shape=jax.ShapeDtypeStruct((rows, deep), BF16),
        cost_estimate=cost(4 * rows * deep * owners * size, 16e6, rows * owners * size),
        compiler_params=params(),
        name="encode",
    )(slot, arrived, gathered)


def attend(queries, keys, values, allowed, scale):
    scores = [
        jnp.where(allowed, lax.dot_general(q, k, NT, preferred_element_type=F32), -jnp.inf)
        for q, k in zip(queries, keys)
    ]
    scores = jnp.concatenate(scores, axis=0)
    probs = jnp.exp2((scores - jnp.max(scores, axis=-1, keepdims=True)) * scale)
    total = jnp.sum(probs, axis=-1, keepdims=True)
    probs = probs.astype(BF16)
    rows = queries[0].shape[0]
    summed = [
        jnp.dot(probs[n * rows : (n + 1) * rows], v, preferred_element_type=F32)
        for n, v in enumerate(values)
    ]
    return jnp.concatenate(summed, axis=0) / total


def cross_kernel(scale, normed, gathered, query, out, sent, weights, sem):
    d = HEAD_DIM
    span = NEIGH * STRETCH
    groups = gathered.shape[0] // 2
    copies = [
        [
            pltpu.make_async_copy(
                gathered.at[part * groups + j, : 2 * d, :],
                weights.at[j, part * 2 * d : (part + 1) * 2 * d, :],
                sem.at[j, part],
            )
            for part in range(2)
        ]
        for j in range(groups)
    ]
    for pair in copies:
        for copy in pair:
            copy.start()
    for pair in copies:
        for copy in pair:
            copy.wait()
    at_row = lax.broadcasted_iota(jnp.int32, (2 * STRETCH, 2 * span), 0)
    at_key = lax.broadcasted_iota(jnp.int32, (2 * STRETCH, 2 * span), 1)
    allowed = (at_row >= STRETCH) == (at_key >= span)
    blocks = range(normed.shape[0] // (2 * span))

    def project(j):
        return lax.dot_general(
            normed[...], weights[j], NT, preferred_element_type=F32
        ).astype(BF16)

    pairs = project(0)
    for j in range(groups):
        later = project(j + 1) if j + 1 < groups else None
        for t in range(2):
            lanes = slice((2 * j + t) * d, (2 * j + t + 1) * d)
            result = attend(
                [query[2 * b * STRETCH : 2 * (b + 1) * STRETCH, lanes] for b in blocks],
                [pairs[2 * b * span : 2 * (b + 1) * span, t * d : (t + 1) * d] for b in blocks],
                [pairs[2 * b * span : 2 * (b + 1) * span, (2 + t) * d : (3 + t) * d] for b in blocks],
                allowed,
                scale,
            )
            result = pltpu.roll(result, STRETCH - 1, 0)
            out[:, lanes] = result.astype(BF16)
            sent[:, lanes] = result[:STRETCH].astype(BF16)
        pairs = later


def cross(normed, gathered, query):
    rows, width = query.shape
    d = HEAD_DIM
    deep = normed.shape[1]
    groups = gathered.shape[0] // 2
    return pl.pallas_call(
        functools.partial(cross_kernel, LOG2E / math.sqrt(d)),
        in_specs=[VMEM, ANY, VMEM],
        out_specs=[VMEM, VMEM],
        out_shape=[
            jax.ShapeDtypeStruct(query.shape, BF16),
            jax.ShapeDtypeStruct((STRETCH, width), BF16),
        ],
        scratch_shapes=[
            pltpu.VMEM((groups, 4 * d, deep), BF16),
            pltpu.SemaphoreType.DMA((groups, 2)),
        ],
        cost_estimate=cost(4 * normed.shape[0] * deep * width, 12e6, 2 * rows * width),
        compiler_params=params(),
        name="cross",
    )(normed, gathered, query)


def mend_kernel(own, before, out):
    last = lax.broadcasted_iota(jnp.int32, own.shape, 0) == STRETCH - 1
    out[...] = jnp.where(last, own[...].astype(F32), before[...].astype(F32)).astype(BF16)


def mend(own, before):
    block = pl.BlockSpec(before.shape, lambda i: (0, 0))
    return pl.pallas_call(
        mend_kernel,
        grid=(1,),
        in_specs=[block, block],
        out_specs=block,
        out_shape=jax.ShapeDtypeStruct(own.shape, BF16),
        input_output_aliases={0: 0},
        cost_estimate=cost(0, 6 * math.prod(before.shape)),
        compiler_params=params(),
        name="mend",
    )(own, before)


def partners(chips):
    place = lax.axis_index("seq")
    chip, core = lax.div(place, 2), lax.rem(place, 2)
    reached, reaching = [], []
    for k, f in HOPS:
        side = 1 - core if f else core
        reached.append(side * chips + lax.rem(chip + k, chips))
        reaching.append(lax.rem(chip + chips - k, chips) * 2 + side)
    return reached, reaching


def pack_kernel(chips, query, key, value, *rest):
    count = len(HOPS)
    parts, held, sem = rest[:count], rest[count], rest[count + 1]
    block = parts[0].shape[2]
    reached, _ = partners(chips)
    reads, writes = [], []
    for n in (*range(1, count), 0):
        columns = pl.ds(pl.multiple_of(reached[n] * block, block), block)
        for a, source in enumerate((query, key, value)):
            reads.append(
                pltpu.make_async_copy(source.at[:, columns], held.at[n, a], sem.at[0, n, a])
            )
            writes.append(pltpu.make_async_copy(held.at[n, a], parts[n].at[a], sem.at[1, n, a]))
    relay(reads, writes)


def pack(chips, query, key, value):
    rows, width = query.shape
    count = len(HOPS)
    shape = (3, rows, width // count)
    return pl.pallas_call(
        functools.partial(pack_kernel, chips),
        in_specs=[ANY] * 3,
        out_specs=[ANY] * count,
        scratch_shapes=[pltpu.VMEM((count, *shape), BF16), pltpu.SemaphoreType.DMA((2, count, 3))],
        out_shape=[jax.ShapeDtypeStruct(shape, BF16)] * count,
        cost_estimate=cost(0, 12 * rows * width),
        compiler_params=params(),
        name="pack",
    )(query, key, value)


def self_kernel(chips, scale, *refs):
    count = len(HOPS)
    _, source = partners(chips)
    parts, outs = refs[:count], refs[count : 2 * count]
    query, key, value, result = refs[2 * count :]
    rows = parts[0].shape[1]
    d = HEAD_DIM
    for n in range(count):
        place = pl.ds(pl.multiple_of(source[n] * rows, rows), rows)
        query[place, :] = parts[n][0]
        key[place, :] = parts[n][1]
        value[place, :d] = parts[n][2]
    value[:, d:] = jnp.ones((count * rows, d), BF16)
    at_row = lax.broadcasted_iota(jnp.int32, (rows, rows), 0)
    at_key = lax.broadcasted_iota(jnp.int32, (rows, rows), 1)
    allowed = at_key <= at_row
    for i in range(count):
        low, high = i * rows, (i + 1) * rows
        block = query[low:high, :]
        scores = lax.dot_general(block, key[low:high, :], NT, preferred_element_type=F32)
        scores = jnp.where(allowed, scores, -jnp.inf)
        if i:
            left = lax.dot_general(block, key[:low, :], NT, preferred_element_type=F32)
            scores = jnp.concatenate([left, scores], axis=1)
        best = jnp.max(scores, axis=-1, keepdims=True)
        probs = jnp.exp2((scores - best) * scale).astype(BF16)
        summed = jnp.dot(probs, value[:high, :], preferred_element_type=F32)
        result[low:high, :] = (summed[:, :d] / summed[:, d:]).astype(BF16)
    for n in range(count):
        place = pl.ds(pl.multiple_of(source[n] * rows, rows), rows)
        outs[n][...] = result[place, :]


def self_attention(chips, parts):
    count = len(HOPS)
    _, rows, width = parts[0].shape
    d = HEAD_DIM
    length = count * rows
    return pl.pallas_call(
        functools.partial(self_kernel, chips, LOG2E / math.sqrt(d)),
        grid=(width // d,),
        in_specs=[pl.BlockSpec((3, rows, d), lambda h: (0, 0, h))] * count,
        out_specs=[pl.BlockSpec((rows, d), lambda h: (0, h))] * count,
        scratch_shapes=[
            pltpu.VMEM((length, d), BF16),
            pltpu.VMEM((length, d), BF16),
            pltpu.VMEM((length, 2 * d), BF16),
            pltpu.VMEM((length, d), BF16),
        ],
        out_shape=[jax.ShapeDtypeStruct((rows, width), BF16)] * count,
        cost_estimate=cost(3 * length * length * d * 2, 8e6, length * length),
        compiler_params=params(),
        name="causal",
    )(*parts)


def unpack_kernel(chips, *refs):
    parts, out = refs[:-1], refs[-1]
    block = parts[0].shape[1]
    reached, _ = partners(chips)
    for n, part in enumerate(parts):
        out[:, pl.ds(pl.multiple_of(reached[n] * block, block), block)] = part[...]


def unpack(chips, parts):
    rows, block = parts[0].shape
    count = len(parts)
    return pl.pallas_call(
        functools.partial(unpack_kernel, chips),
        in_specs=[VMEM] * count,
        out_specs=VMEM,
        out_shape=jax.ShapeDtypeStruct((rows, block * count), BF16),
        cost_estimate=cost(0, 4 * rows * block * count),
        compiler_params=params(),
        name="unpack",
    )(*parts)


def requests_of(retrieval_shard, retrieval_row):
    shard_list = retrieval_shard.reshape(-1)
    row_list = retrieval_row.reshape(-1)
    owners = lax.axis_size("db")
    order = jnp.arange(shard_list.shape[0])
    earlier = (order[:, None] > order[None, :]) & (shard_list[:, None] == shard_list[None, :])
    rank = jnp.sum(earlier.astype(jnp.int32), axis=1)
    slot = shard_list * CAP + rank
    hits = jnp.arange(owners * CAP)[:, None] == slot[None, :]
    wanted = jnp.sum(jnp.where(hits, row_list[None, :], 0), axis=1).reshape(owners, CAP)
    return slot, wanted


def shards(
    self_query,
    self_key,
    self_value,
    cross_query,
    retrieval_shard,
    retrieval_row,
    database,
    ffn_in,
    ffn_out,
    cross_projection,
):
    owners = lax.axis_size("db")
    count = lax.axis_size("seq")
    chips = count // 2
    size, deep = ffn_out.shape
    together = lax.optimization_barrier

    weights = jnp.concatenate([cross_projection.T, ffn_in.T, ffn_out], axis=0)
    share = weights.shape[0] // count
    part = lax.dynamic_slice_in_dim(weights, lax.axis_index("seq") * share, share, 0)
    gathered = lax.all_gather(part, ("db", "seq"), axis=0, tiled=True).reshape(owners, -1, deep)

    slot, wanted = requests_of(retrieval_shard, retrieval_row)
    asked = lax.all_to_all(wanted, "db", split_axis=0, concat_axis=0, tiled=True)
    self_query, self_key, self_value, _ = together((self_query, self_key, self_value, wanted))
    parts = pack(chips, self_query, self_key, self_value)
    asked, *parts = together((asked, *parts))
    parts = [parts[0]] + [hop(p, k, f) for p, (k, f) in zip(parts[1:], HOPS[1:])]

    found = fetch(asked.reshape(-1), database)
    arrived = lax.all_to_all(found, "db", split_axis=0, concat_axis=0, tiled=True)
    ahead = lax.ppermute(cross_query[:STRETCH], "seq", [(i, i - 1) for i in range(1, count)])

    done = self_attention(chips, parts)
    back = [done[0]] + [hop(p, chips - k, f) for p, (k, f) in zip(done[1:], HOPS[1:])]

    shifted = jnp.concatenate([cross_query[STRETCH - 1 :], ahead[: STRETCH - 1]], axis=0)
    gathered, shifted, arrived, *back = together((gathered, shifted, arrived, *back))
    normed = encode(slot, arrived, gathered, cross_projection.shape[1], size)
    own, sent = cross(normed, gathered, shifted)
    before = lax.ppermute(sent, "seq", [(i, i + 1) for i in range(count - 1)])
    own, *back = together((own, *back))
    self_attended = unpack(chips, back)
    cross_attended = mend(own, before)
    return (self_attended, cross_attended)


def solution(mesh):
    in_specs = (
        P(("db", "seq"), None),
        P(("db", "seq"), None),
        P(("db", "seq"), None),
        P(("db", "seq"), None),
        P(("db", "seq"), None),
        P(("db", "seq"), None),
        P("db", None, None),
        P(None, "db"),
        P("db", None),
        P(None, "db"),
    )
    out_specs = (P(("db", "seq"), None), P(("db", "seq"), None))
    return jax.shard_map(shards, mesh=mesh, in_specs=in_specs, out_specs=out_specs, check_vma=False)
```

```python
import functools
import math

import jax
import jax.numpy as jnp
from jax import lax
from jax.experimental import pallas as pl
from jax.experimental.pallas import tpu as pltpu
from jax.sharding import PartitionSpec as P

HEADS = 16
HEAD_DIM = 128
STRETCH = 64
NEIGH = 2
CAP = 2
LOG2E = 1.4426950408889634
BF16 = jnp.bfloat16
F32 = jnp.float32
NT = (((1,), (1,)), ((), ()))
ANY = pl.BlockSpec(memory_space=pl.ANY)
VMEM = pl.BlockSpec(memory_space=pltpu.VMEM)
HOPS = (0, 2, 1, 3)


def cost(flops, size, exps=0):
    return pl.CostEstimate(flops=int(flops), bytes_accessed=int(size), transcendentals=int(exps))


def params(mib=56, **more):
    return pltpu.CompilerParams(vmem_limit_bytes=mib << 20, **more)


def hop(value, chips, flip):
    count = lax.axis_size("seq")
    pairs = [(i, ((i + 2 * chips) % count) ^ flip) for i in range(count)]
    return lax.ppermute(value, "seq", pairs)


def run_copies(copies):
    for copy in copies:
        copy.start()
    for copy in copies:
        copy.wait()


def rms(wide):
    return wide * lax.rsqrt(jnp.mean(wide * wide, axis=-1, keepdims=True) + 1e-06)


def relay(reads, writes):
    for copy in reads:
        copy.start()
    for read, write in zip(reads, writes):
        read.wait()
        write.start()
    for copy in writes:
        copy.wait()


def fetch_kernel(asked, database, found, held, sem):
    last = database.shape[0] - 1
    count = found.shape[0]
    relay(
        [
            pltpu.make_async_copy(
                database.at[jnp.clip(asked[i], 0, last)], held.at[i], sem.at[0, i]
            )
            for i in range(count)
        ],
        [pltpu.make_async_copy(held.at[i], found.at[i], sem.at[1, i]) for i in range(count)],
    )


def fetch(asked, database):
    slots = asked.shape[0]
    shape = (slots, *database.shape[1:])
    return pl.pallas_call(
        fetch_kernel,
        grid_spec=pltpu.PrefetchScalarGridSpec(
            num_scalar_prefetch=1,
            grid=(1,),
            in_specs=[ANY],
            out_specs=ANY,
            scratch_shapes=[pltpu.VMEM(shape, BF16), pltpu.SemaphoreType.DMA((2, slots))],
        ),
        out_shape=jax.ShapeDtypeStruct(shape, BF16),
        cost_estimate=cost(0, 4 * math.prod(shape)),
        compiler_params=params(),
        name="fetch",
    )(asked, database)


def half_kernel(half, ffn_in, ffn_out, projection, out):
    core = lax.rem(lax.axis_index("seq"), 2)
    rows = pl.ds(pl.multiple_of(core * half, 16), half)
    out[:half, :] = ffn_in[rows, :]
    out[half : 2 * half, :] = ffn_out[rows, :]
    columns = pl.ds(pl.multiple_of(core * HEAD_DIM, HEAD_DIM), HEAD_DIM)
    out[2 * half :, :] = jnp.transpose(projection[:, columns])


def half_of(ffn_in, ffn_out, projection):
    rows, deep = ffn_out.shape
    return pl.pallas_call(
        functools.partial(half_kernel, rows // 2),
        in_specs=[VMEM] * 3,
        out_specs=VMEM,
        out_shape=jax.ShapeDtypeStruct((rows + HEAD_DIM, deep), BF16),
        cost_estimate=cost(0, 4 * rows * deep),
        compiler_params=params(),
        name="half",
    )(ffn_in.T, ffn_out, projection)


def rows_of(gathered, target, first, size, place, sem):
    return [
        pltpu.make_async_copy(
            gathered.at[b, first : first + size, :], target.at[pl.ds(place(b), size), :], sem.at[b]
        )
        for b in range(gathered.shape[0])
    ]


def feed_forward(normed, w_in, w_out, hidden):
    step = 256
    for j in range(w_in.shape[0] // step):
        rows = slice(j * step, (j + 1) * step)
        wide = lax.dot_general(normed[...], w_in[rows, :], NT, preferred_element_type=F32)
        hidden[:, rows] = jax.nn.gelu(wide, approximate=True).astype(BF16)
    return jnp.dot(hidden[...], w_out[...], preferred_element_type=F32)


def encode_kernel(slot, arrived, gathered, total, normed, x, w_in, w_out, hidden, x_sem, sem):
    tokens = arrived.shape[1]
    half = w_in.shape[0] // gathered.shape[0]
    copies = [
        pltpu.make_async_copy(
            arrived.at[slot[i]], x.at[i * tokens : (i + 1) * tokens, :], x_sem.at[i]
        )
        for i in range(x.shape[0] // tokens)
    ]
    copies += rows_of(gathered, w_in, 0, half, lambda b: b * half, sem.at[0])
    copies += rows_of(gathered, w_out, half, half, lambda b: b * half, sem.at[1])
    run_copies(copies)
    normed[...] = rms(x[...].astype(F32)).astype(BF16)
    total[...] = x[...].astype(F32) + feed_forward(normed, w_in, w_out, hidden)


def encode(slot, arrived, gathered, half):
    requests = slot.shape[0]
    rows, deep = requests * arrived.shape[1], arrived.shape[2]
    owners = gathered.shape[0]
    whole = pl.BlockSpec((rows, deep), lambda i, s: (0, 0))
    return pl.pallas_call(
        encode_kernel,
        grid_spec=pltpu.PrefetchScalarGridSpec(
            num_scalar_prefetch=1,
            grid=(1,),
            in_specs=[ANY, ANY],
            out_specs=[whole, whole],
            scratch_shapes=[
                pltpu.VMEM((rows, deep), BF16),
                pltpu.VMEM((owners * half, deep), BF16),
                pltpu.VMEM((owners * half, deep), BF16),
                pltpu.VMEM((rows, owners * half), BF16),
                pltpu.SemaphoreType.DMA((requests,)),
                pltpu.SemaphoreType.DMA((2, owners)),
            ],
        ),
        out_shape=[
            jax.ShapeDtypeStruct((rows, deep), F32),
            jax.ShapeDtypeStruct((rows, deep), BF16),
        ],
        cost_estimate=cost(5e9, 12e6, 2e6),
        compiler_params=params(),
        name="encode",
    )(slot, arrived, gathered)


def attend(queries, keys, values, allowed, scale):
    scores = [
        jnp.where(allowed, lax.dot_general(q, k, NT, preferred_element_type=F32), -jnp.inf)
        for q, k in zip(queries, keys)
    ]
    scores = jnp.concatenate(scores, axis=0)
    probs = jnp.exp2((scores - jnp.max(scores, axis=-1, keepdims=True)) * scale)
    total = jnp.sum(probs, axis=-1, keepdims=True)
    probs = probs.astype(BF16)
    rows = queries[0].shape[0]
    summed = [
        jnp.dot(probs[n * rows : (n + 1) * rows], v, preferred_element_type=F32)
        for n, v in enumerate(values)
    ]
    return jnp.concatenate(summed, axis=0) / total


def cross_kernel(
    scale, half, before, normed_in, mine, other, query, out, sent, normed, w_in, w_out, hidden, w_pair, pairs, sem
):
    d = HEAD_DIM
    core = lax.rem(lax.axis_index("seq"), 2)
    own = lambda b: pl.multiple_of((2 * b + core) * d, d)
    rest = lambda b: pl.multiple_of((2 * b + 1 - core) * d, d)
    copies = rows_of(other, w_in, 0, half, lambda b: b * half, sem.at[0])
    copies += rows_of(other, w_out, half, half, lambda b: b * half, sem.at[1])
    projections = rows_of(mine, w_pair, 2 * half, d, own, sem.at[2])
    projections += rows_of(other, w_pair, 2 * half, d, rest, sem.at[3])
    for copy in copies + projections:
        copy.start()

    for copy in copies:
        copy.wait()
    mixed = feed_forward(normed_in, w_in, w_out, hidden)
    encoded = (before[...] + mixed).astype(BF16).astype(F32)
    for copy in projections:
        copy.wait()
    normed[...] = rms(encoded).astype(BF16)
    step = 512

    for j in range(w_pair.shape[0] // step):
        rows = slice(j * step, (j + 1) * step)
        wide = lax.dot_general(normed[...], w_pair[rows, :], NT, preferred_element_type=F32)
        pairs[:, rows] = wide.astype(BF16)

    span = NEIGH * STRETCH
    width = query.shape[1]
    at_row = lax.broadcasted_iota(jnp.int32, (2 * STRETCH, 2 * span), 0)
    at_key = lax.broadcasted_iota(jnp.int32, (2 * STRETCH, 2 * span), 1)
    allowed = (at_row >= STRETCH) == (at_key >= span)
    blocks = normed.shape[0] // (2 * span)
    together = 4
    for h in range(0, width // d, together):
        heads = [(t, b) for t in range(h, h + together) for b in range(blocks)]
        result = attend(
            [query[2 * b * STRETCH : 2 * (b + 1) * STRETCH, t * d : (t + 1) * d] for t, b in heads],
            [pairs[2 * b * span : 2 * (b + 1) * span, t * d : (t + 1) * d] for t, b in heads],
            [
                pairs[2 * b * span : 2 * (b + 1) * span, width + t * d : width + (t + 1) * d]
                for t, b in heads
            ],
            allowed,
            scale,
        )
        rows = query.shape[0]
        for n in range(together):
            lanes = slice((h + n) * d, (h + n + 1) * d)
            moved = pltpu.roll(result[n * rows : (n + 1) * rows], STRETCH - 1, 0)
            out[:, lanes] = moved.astype(BF16)
            sent[:, lanes] = moved[:STRETCH].astype(BF16)


def cross(before, normed_in, mine, other, query, half):
    rows, width = query.shape
    d = HEAD_DIM
    owners, _, deep = mine.shape
    tokens = before.shape[0]
    return pl.pallas_call(
        functools.partial(cross_kernel, LOG2E / math.sqrt(d), half),
        in_specs=[VMEM, VMEM, ANY, ANY, VMEM],
        out_specs=[VMEM, VMEM],
        scratch_shapes=[
            pltpu.VMEM((tokens, deep), BF16),
            pltpu.VMEM((owners * half, deep), BF16),
            pltpu.VMEM((owners * half, deep), BF16),
            pltpu.VMEM((tokens, owners * half), BF16),
            pltpu.VMEM((2 * width, deep), BF16),
            pltpu.VMEM((tokens, 2 * width), BF16),
            pltpu.SemaphoreType.DMA((4, owners)),
        ],
        out_shape=[
            jax.ShapeDtypeStruct(query.shape, BF16),
            jax.ShapeDtypeStruct((STRETCH, width), BF16),
        ],
        cost_estimate=cost(12e9, 20e6, 4e6),
        compiler_params=params(60),
        name="cross",
    )(before, normed_in, mine, other, query)


def mend_kernel(own, before, out):
    last = lax.broadcasted_iota(jnp.int32, own.shape, 0) == STRETCH - 1
    out[...] = jnp.where(last, own[...].astype(F32), before[...].astype(F32)).astype(BF16)


def mend(own, before):
    block = pl.BlockSpec(before.shape, lambda i: (0, 0))
    return pl.pallas_call(
        mend_kernel,
        grid=(1,),
        in_specs=[block, block],
        out_specs=block,
        out_shape=jax.ShapeDtypeStruct(own.shape, BF16),
        input_output_aliases={0: 0},
        cost_estimate=cost(0, 6 * math.prod(before.shape)),
        compiler_params=params(),
        name="mend",
    )(own, before)


def partners(chips):
    place = lax.axis_index("seq")
    chip, core = lax.div(place, 2), lax.rem(place, 2)
    sides = (core, 1 - core)
    reached = [[side * chips + lax.rem(chip + k, chips) for side in sides] for k in HOPS]
    reaching = [[lax.rem(chip + chips - k, chips) * 2 + side for side in sides] for k in HOPS]
    return reached, reaching


def pack_kernel(chips, query, key, value, *rest):
    count = len(HOPS)
    parts, held, sem = rest[:count], rest[count], rest[count + 1]
    block = parts[0].shape[3]
    reached, _ = partners(chips)
    reads, writes = [], []
    for n in (*range(1, count), 0):
        for f in range(2):
            columns = pl.ds(pl.multiple_of(reached[n][f] * block, block), block)
            for a, source in enumerate((query, key, value)):
                place = held.at[n, f, a]
                reads.append(
                    pltpu.make_async_copy(source.at[:, columns], place, sem.at[0, n, f, a])
                )
                writes.append(
                    pltpu.make_async_copy(place, parts[n].at[f, a], sem.at[1, n, f, a])
                )
    relay(reads, writes)


def pack(chips, query, key, value):
    rows, width = query.shape
    count = len(HOPS)
    shape = (2, 3, rows, width // (2 * count))
    return pl.pallas_call(
        functools.partial(pack_kernel, chips),
        in_specs=[ANY] * 3,
        out_specs=[ANY] * count,
        scratch_shapes=[pltpu.VMEM((count, *shape), BF16), pltpu.SemaphoreType.DMA((2, count, 2, 3))],
        out_shape=[jax.ShapeDtypeStruct(shape, BF16)] * count,
        cost_estimate=cost(0, 12 * rows * width),
        compiler_params=params(),
        name="pack",
    )(query, key, value)


def self_kernel(chips, scale, *refs):
    hops = len(HOPS)
    count = 2 * hops
    parts, outs = refs[:count], refs[count : count + hops]
    query, key, value, result = refs[count + hops :]
    _, source = partners(chips)
    rows = parts[0].shape[2]
    d = HEAD_DIM
    places = [
        [pl.ds(pl.multiple_of(source[n][f] * rows, rows), rows) for f in range(2)]
        for n in range(hops)
    ]
    for n in range(hops):
        for f in range(2):
            part, place = parts[f * hops + n], places[n][f]
            query[place, :] = part[0, 0]
            key[place, :] = part[0, 1]
            value[place, :d] = part[0, 2]
    value[:, d:] = jnp.ones((count * rows, d), BF16)
    at_row = lax.broadcasted_iota(jnp.int32, (rows, rows), 0)
    at_key = lax.broadcasted_iota(jnp.int32, (rows, rows), 1)
    allowed = at_key <= at_row
    for i in range(count):
        low, high = i * rows, (i + 1) * rows
        block = query[low:high, :]
        scores = lax.dot_general(block, key[low:high, :], NT, preferred_element_type=F32)
        scores = jnp.where(allowed, scores, -jnp.inf)
        if i:
            left = lax.dot_general(block, key[:low, :], NT, preferred_element_type=F32)
            scores = jnp.concatenate([left, scores], axis=1)
        best = jnp.max(scores, axis=-1, keepdims=True)
        probs = jnp.exp2((scores - best) * scale).astype(BF16)
        summed = jnp.dot(probs, value[:high, :], preferred_element_type=F32)
        result[low:high, :] = (summed[:, :d] / summed[:, d:]).astype(BF16)
    for n in range(hops):
        for f in range(2):
            outs[n][f] = result[places[n][f], :]


def self_attention(chips, same, flipped):
    hops = len(HOPS)
    _, _, rows, width = same[0].shape
    d = HEAD_DIM
    length = 2 * hops * rows
    at = lambda f: pl.BlockSpec((1, 3, rows, d), lambda h: (f, 0, 0, h))
    return pl.pallas_call(
        functools.partial(self_kernel, chips, LOG2E / math.sqrt(d)),
        grid=(width // d,),
        in_specs=[at(0)] * hops + [at(1)] * hops,
        out_specs=[pl.BlockSpec((2, rows, d), lambda h: (0, 0, h))] * hops,
        scratch_shapes=[
            pltpu.VMEM((length, d), BF16),
            pltpu.VMEM((length, d), BF16),
            pltpu.VMEM((length, 2 * d), BF16),
            pltpu.VMEM((length, d), BF16),
        ],
        out_shape=[jax.ShapeDtypeStruct((2, rows, width), BF16)] * hops,
        cost_estimate=cost(7e9, 8e6, length * length),
        compiler_params=params(),
        name="causal",
    )(*same, *flipped)


def unpack_kernel(chips, *refs):
    hops = len(HOPS)
    parts, out = refs[:-1], refs[-1]
    block = parts[0].shape[2]
    reached, _ = partners(chips)
    for n in range(hops):
        for f in range(2):
            columns = pl.ds(pl.multiple_of(reached[n][f] * block, block), block)
            out[:, columns] = parts[f * hops + n][0]


def unpack(chips, same, flipped):
    hops = len(HOPS)
    _, rows, block = same[0].shape
    at = lambda f: pl.BlockSpec((1, rows, block), lambda i: (f, 0, 0))
    shape = (rows, 2 * hops * block)
    return pl.pallas_call(
        functools.partial(unpack_kernel, chips),
        grid=(1,),
        in_specs=[at(0)] * hops + [at(1)] * hops,
        out_specs=pl.BlockSpec(shape, lambda i: (0, 0)),
        out_shape=jax.ShapeDtypeStruct(shape, BF16),
        cost_estimate=cost(0, 4 * math.prod(shape)),
        compiler_params=params(),
        name="unpack",
    )(*same, *flipped)


def requests_of(retrieval_shard, retrieval_row):
    shard_list = retrieval_shard.reshape(-1)
    row_list = retrieval_row.reshape(-1)
    owners = lax.axis_size("db")
    order = jnp.arange(shard_list.shape[0])
    earlier = (order[:, None] > order[None, :]) & (shard_list[:, None] == shard_list[None, :])
    rank = jnp.sum(earlier.astype(jnp.int32), axis=1)
    slot = shard_list * CAP + rank
    hits = jnp.arange(owners * CAP)[:, None] == slot[None, :]
    wanted = jnp.sum(jnp.where(hits, row_list[None, :], 0), axis=1).reshape(owners, CAP)
    return slot, wanted


def shards(
    self_query,
    self_key,
    self_value,
    cross_query,
    retrieval_shard,
    retrieval_row,
    database,
    ffn_in,
    ffn_out,
    cross_projection,
):
    owners = lax.axis_size("db")
    count = lax.axis_size("seq")
    chips = count // 2
    half, deep = ffn_out.shape[0] // 2, ffn_out.shape[1]
    together = lax.optimization_barrier

    part = half_of(ffn_in, ffn_out, cross_projection)
    mine = lax.all_gather(part, "db", axis=0, tiled=True).reshape(owners, -1, deep)

    slot, wanted = requests_of(retrieval_shard, retrieval_row)
    asked = lax.all_to_all(wanted, "db", split_axis=0, concat_axis=0, tiled=True)
    self_query, self_key, self_value, _ = together((self_query, self_key, self_value, wanted))
    parts = pack(chips, self_query, self_key, self_value)
    same = [parts[0]] + [hop(p, k, 0) for p, k in zip(parts[1:], HOPS[1:])]

    found = fetch(asked.reshape(-1), database)
    *same, _ = together((*same, found))
    flipped = [hop(p, 0, 1) for p in same]
    arrived = lax.all_to_all(found, "db", split_axis=0, concat_axis=0, tiled=True)
    ahead = lax.ppermute(cross_query[:STRETCH], "seq", [(i, i - 1) for i in range(1, count)])

    done = self_attention(chips, same, flipped)
    same = [done[0]] + [hop(p, chips - k, 0) for p, k in zip(done[1:], HOPS[1:])]
    flipped = [hop(p, 0, 1) for p in same]
    self_attended = unpack(chips, same, flipped)

    shifted = jnp.concatenate([cross_query[STRETCH - 1 :], ahead[: STRETCH - 1]], axis=0)
    mine, shifted, arrived, _ = together((mine, shifted, arrived, self_attended))
    other = hop(mine, 0, 1)
    total, normed = encode(slot, arrived, mine, half)
    own, sent = cross(total, normed, mine, other, shifted, half)
    before = lax.ppermute(sent, "seq", [(i, i + 1) for i in range(count - 1)])
    cross_attended = mend(own, before)
    return (self_attended, cross_attended)


def solution(mesh):
    in_specs = (
        P(("db", "seq"), None),
        P(("db", "seq"), None),
        P(("db", "seq"), None),
        P(("db", "seq"), None),
        P(("db", "seq"), None),
        P(("db", "seq"), None),
        P("db", None, None),
        P(None, "db"),
        P("db", None),
        P(None, "db"),
    )
    out_specs = (P(("db", "seq"), None), P(("db", "seq"), None))
    return jax.shard_map(shards, mesh=mesh, in_specs=in_specs, out_specs=out_specs, check_vma=False)
```

```python
import functools
import math

import jax
import jax.numpy as jnp
from jax import lax
from jax.experimental import pallas as pl
from jax.experimental.pallas import tpu as pltpu
from jax.sharding import PartitionSpec as P

HEADS = 16
HEAD_DIM = 128
STRETCH = 64
NEIGH = 2
CAP = 2
LOG2E = 1.4426950408889634
BF16 = jnp.bfloat16
F32 = jnp.float32
NT = (((1,), (1,)), ((), ()))
ANY = pl.BlockSpec(memory_space=pl.ANY)
VMEM = pl.BlockSpec(memory_space=pltpu.VMEM)
HOPS = (0, 2, 1, 3)


def cost(flops, size, exps=0):
    return pl.CostEstimate(flops=int(flops), bytes_accessed=int(size), transcendentals=int(exps))


def params(mib=56, **more):
    return pltpu.CompilerParams(vmem_limit_bytes=mib << 20, **more)


def hop(value, chips, flip):
    count = lax.axis_size("seq")
    pairs = [(i, ((i + 2 * chips) % count) ^ flip) for i in range(count)]
    return lax.ppermute(value, "seq", pairs)


def run_copies(copies):
    for copy in copies:
        copy.start()
    for copy in copies:
        copy.wait()


def rms(wide):
    return wide * lax.rsqrt(jnp.mean(wide * wide, axis=-1, keepdims=True) + 1e-06)


def relay(reads, writes):
    for copy in reads:
        copy.start()
    for read, write in zip(reads, writes):
        read.wait()
        write.start()
    for copy in writes:
        copy.wait()


def fetch_kernel(asked, database, found, held, sem):
    last = database.shape[0] - 1
    count = found.shape[0]
    relay(
        [
            pltpu.make_async_copy(
                database.at[jnp.clip(asked[i // CAP, i % CAP], 0, last)], held.at[i], sem.at[0, i]
            )
            for i in range(count)
        ],
        [pltpu.make_async_copy(held.at[i], found.at[i], sem.at[1, i]) for i in range(count)],
    )


def fetch(asked, database):
    slots = math.prod(asked.shape)
    shape = (slots, *database.shape[1:])
    return pl.pallas_call(
        fetch_kernel,
        grid_spec=pltpu.PrefetchScalarGridSpec(
            num_scalar_prefetch=1,
            grid=(1,),
            in_specs=[ANY],
            out_specs=ANY,
            scratch_shapes=[pltpu.VMEM(shape, BF16), pltpu.SemaphoreType.DMA((2, slots))],
        ),
        out_shape=jax.ShapeDtypeStruct(shape, BF16),
        cost_estimate=cost(0, 4 * math.prod(shape)),
        compiler_params=params(),
        name="fetch",
    )(asked, database)


def half_kernel(half, ffn_in, ffn_out, projection, out):
    core = lax.rem(lax.axis_index("seq"), 2)
    rows = pl.ds(pl.multiple_of(core * half, 16), half)
    out[:half, :] = ffn_in[rows, :]
    out[half : 2 * half, :] = ffn_out[rows, :]
    columns = pl.ds(pl.multiple_of(core * HEAD_DIM, HEAD_DIM), HEAD_DIM)
    out[2 * half :, :] = jnp.transpose(projection[:, columns])


def half_of(ffn_in, ffn_out, projection):
    rows, deep = ffn_out.shape
    return pl.pallas_call(
        functools.partial(half_kernel, rows // 2),
        in_specs=[VMEM] * 3,
        out_specs=VMEM,
        out_shape=jax.ShapeDtypeStruct((rows + HEAD_DIM, deep), BF16),
        cost_estimate=cost(0, 4 * rows * deep),
        compiler_params=params(),
        name="half",
    )(ffn_in.T, ffn_out, projection)


def rows_of(gathered, target, first, size, place, sem):
    return [
        pltpu.make_async_copy(
            gathered.at[b, first : first + size, :], target.at[pl.ds(place(b), size), :], sem.at[b]
        )
        for b in range(gathered.shape[0])
    ]


def feed_forward(normed, w_in, w_out, hidden):
    step = 256
    for j in range(w_in.shape[0] // step):
        rows = slice(j * step, (j + 1) * step)
        wide = lax.dot_general(normed[...], w_in[rows, :], NT, preferred_element_type=F32)
        hidden[:, rows] = jax.nn.gelu(wide, approximate=True).astype(BF16)
    return jnp.dot(hidden[...], w_out[...], preferred_element_type=F32)


def encode_kernel(slot, arrived, gathered, total, normed, x, w_in, w_out, hidden, x_sem, sem):
    tokens = arrived.shape[1]
    half = w_in.shape[0] // gathered.shape[0]
    copies = [
        pltpu.make_async_copy(
            arrived.at[slot[i]], x.at[i * tokens : (i + 1) * tokens, :], x_sem.at[i]
        )
        for i in range(x.shape[0] // tokens)
    ]
    copies += rows_of(gathered, w_in, 0, half, lambda b: b * half, sem.at[0])
    copies += rows_of(gathered, w_out, half, half, lambda b: b * half, sem.at[1])
    run_copies(copies)
    normed[...] = rms(x[...].astype(F32)).astype(BF16)
    total[...] = x[...].astype(F32) + feed_forward(normed, w_in, w_out, hidden)


def encode(slot, arrived, gathered, half):
    requests = slot.shape[0]
    rows, deep = requests * arrived.shape[1], arrived.shape[2]
    owners = gathered.shape[0]
    whole = pl.BlockSpec((rows, deep), lambda i, s: (0, 0))
    return pl.pallas_call(
        encode_kernel,
        grid_spec=pltpu.PrefetchScalarGridSpec(
            num_scalar_prefetch=1,
            grid=(1,),
            in_specs=[ANY, ANY],
            out_specs=[whole, whole],
            scratch_shapes=[
                pltpu.VMEM((rows, deep), BF16),
                pltpu.VMEM((owners * half, deep), BF16),
                pltpu.VMEM((owners * half, deep), BF16),
                pltpu.VMEM((rows, owners * half), BF16),
                pltpu.SemaphoreType.DMA((requests,)),
                pltpu.SemaphoreType.DMA((2, owners)),
            ],
        ),
        out_shape=[
            jax.ShapeDtypeStruct((rows, deep), F32),
            jax.ShapeDtypeStruct((rows, deep), BF16),
        ],
        cost_estimate=cost(5e9, 12e6, 2e6),
        compiler_params=params(),
        name="encode",
    )(slot, arrived, gathered)


def attend(queries, keys, values, allowed, scale):
    scores = [
        jnp.where(allowed, lax.dot_general(q, k, NT, preferred_element_type=F32), -jnp.inf)
        for q, k in zip(queries, keys)
    ]
    scores = jnp.concatenate(scores, axis=0)
    probs = jnp.exp2((scores - jnp.max(scores, axis=-1, keepdims=True)) * scale)
    total = jnp.sum(probs, axis=-1, keepdims=True)
    probs = probs.astype(BF16)
    rows = queries[0].shape[0]
    summed = [
        jnp.dot(probs[n * rows : (n + 1) * rows], v, preferred_element_type=F32)
        for n, v in enumerate(values)
    ]
    return jnp.concatenate(summed, axis=0) / total


def cross_kernel(
    scale, half, before, normed_in, mine, other, query, out, sent, normed, w_in, w_out, hidden, w_pair, pairs, sem
):
    d = HEAD_DIM
    core = lax.rem(lax.axis_index("seq"), 2)
    own = lambda b: pl.multiple_of((2 * b + core) * d, d)
    rest = lambda b: pl.multiple_of((2 * b + 1 - core) * d, d)
    copies = rows_of(other, w_in, 0, half, lambda b: b * half, sem.at[0])
    copies += rows_of(other, w_out, half, half, lambda b: b * half, sem.at[1])
    projections = rows_of(mine, w_pair, 2 * half, d, own, sem.at[2])
    projections += rows_of(other, w_pair, 2 * half, d, rest, sem.at[3])
    for copy in copies + projections:
        copy.start()

    for copy in copies:
        copy.wait()
    mixed = feed_forward(normed_in, w_in, w_out, hidden)
    encoded = (before[...] + mixed).astype(BF16).astype(F32)
    for copy in projections:
        copy.wait()
    normed[...] = rms(encoded).astype(BF16)
    step = 512

    for j in range(w_pair.shape[0] // step):
        rows = slice(j * step, (j + 1) * step)
        wide = lax.dot_general(normed[...], w_pair[rows, :], NT, preferred_element_type=F32)
        pairs[:, rows] = wide.astype(BF16)

    span = NEIGH * STRETCH
    width = query.shape[1]
    at_row = lax.broadcasted_iota(jnp.int32, (2 * STRETCH, 2 * span), 0)
    at_key = lax.broadcasted_iota(jnp.int32, (2 * STRETCH, 2 * span), 1)
    allowed = (at_row >= STRETCH) == (at_key >= span)
    blocks = normed.shape[0] // (2 * span)
    together = 4
    for h in range(0, width // d, together):
        heads = [(t, b) for t in range(h, h + together) for b in range(blocks)]
        result = attend(
            [query[2 * b * STRETCH : 2 * (b + 1) * STRETCH, t * d : (t + 1) * d] for t, b in heads],
            [pairs[2 * b * span : 2 * (b + 1) * span, t * d : (t + 1) * d] for t, b in heads],
            [
                pairs[2 * b * span : 2 * (b + 1) * span, width + t * d : width + (t + 1) * d]
                for t, b in heads
            ],
            allowed,
            scale,
        )
        rows = query.shape[0]
        for n in range(together):
            lanes = slice((h + n) * d, (h + n + 1) * d)
            moved = pltpu.roll(result[n * rows : (n + 1) * rows], STRETCH - 1, 0)
            out[:, lanes] = moved.astype(BF16)
            sent[:, lanes] = moved[:STRETCH].astype(BF16)


def cross(before, normed_in, mine, other, query, half):
    rows, width = query.shape
    d = HEAD_DIM
    owners, _, deep = mine.shape
    tokens = before.shape[0]
    return pl.pallas_call(
        functools.partial(cross_kernel, LOG2E / math.sqrt(d), half),
        in_specs=[VMEM, VMEM, ANY, ANY, VMEM],
        out_specs=[VMEM, VMEM],
        scratch_shapes=[
            pltpu.VMEM((tokens, deep), BF16),
            pltpu.VMEM((owners * half, deep), BF16),
            pltpu.VMEM((owners * half, deep), BF16),
            pltpu.VMEM((tokens, owners * half), BF16),
            pltpu.VMEM((2 * width, deep), BF16),
            pltpu.VMEM((tokens, 2 * width), BF16),
            pltpu.SemaphoreType.DMA((4, owners)),
        ],
        out_shape=[
            jax.ShapeDtypeStruct(query.shape, BF16),
            jax.ShapeDtypeStruct((STRETCH, width), BF16),
        ],
        cost_estimate=cost(12e9, 20e6, 4e6),
        compiler_params=params(60),
        name="cross",
    )(before, normed_in, mine, other, query)


def mend_kernel(own, before, out):
    last = lax.broadcasted_iota(jnp.int32, own.shape, 0) == STRETCH - 1
    out[...] = jnp.where(last, own[...].astype(F32), before[...].astype(F32)).astype(BF16)


def mend(own, before):
    block = pl.BlockSpec(before.shape, lambda i: (0, 0))
    return pl.pallas_call(
        mend_kernel,
        grid=(1,),
        in_specs=[block, block],
        out_specs=block,
        out_shape=jax.ShapeDtypeStruct(own.shape, BF16),
        input_output_aliases={0: 0},
        cost_estimate=cost(0, 6 * math.prod(before.shape)),
        compiler_params=params(),
        name="mend",
    )(own, before)


def partners(chips):
    place = lax.axis_index("seq")
    chip, core = lax.div(place, 2), lax.rem(place, 2)
    sides = (core, 1 - core)
    reached = [[side * chips + lax.rem(chip + k, chips) for side in sides] for k in HOPS]
    reaching = [[lax.rem(chip + chips - k, chips) * 2 + side for side in sides] for k in HOPS]
    return reached, reaching


def pack_kernel(chips, query, key, value, *rest):
    count = len(HOPS)
    parts, held, sem = rest[:count], rest[count], rest[count + 1]
    block = parts[0].shape[3]
    reached, _ = partners(chips)
    reads, writes = [], []
    for n in (*range(1, count), 0):
        for f in range(2):
            columns = pl.ds(pl.multiple_of(reached[n][f] * block, block), block)
            for a, source in enumerate((query, key, value)):
                place = held.at[n, f, a]
                reads.append(
                    pltpu.make_async_copy(source.at[:, columns], place, sem.at[0, n, f, a])
                )
                writes.append(
                    pltpu.make_async_copy(place, parts[n].at[f, a], sem.at[1, n, f, a])
                )
    relay(reads, writes)


def pack(chips, query, key, value):
    rows, width = query.shape
    count = len(HOPS)
    shape = (2, 3, rows, width // (2 * count))
    return pl.pallas_call(
        functools.partial(pack_kernel, chips),
        in_specs=[ANY] * 3,
        out_specs=[ANY] * count,
        scratch_shapes=[pltpu.VMEM((count, *shape), BF16), pltpu.SemaphoreType.DMA((2, count, 2, 3))],
        out_shape=[jax.ShapeDtypeStruct(shape, BF16)] * count,
        cost_estimate=cost(0, 12 * rows * width),
        compiler_params=params(),
        name="pack",
    )(query, key, value)


def self_kernel(chips, scale, *refs):
    hops = len(HOPS)
    count = 2 * hops
    parts, outs = refs[:count], refs[count : count + hops]
    query, key, value, result = refs[count + hops :]
    _, source = partners(chips)
    rows = parts[0].shape[2]
    d = HEAD_DIM
    places = [
        [pl.ds(pl.multiple_of(source[n][f] * rows, rows), rows) for f in range(2)]
        for n in range(hops)
    ]
    for n in range(hops):
        for f in range(2):
            part, place = parts[f * hops + n], places[n][f]
            query[place, :] = part[0, 0]
            key[place, :] = part[0, 1]
            value[place, :d] = part[0, 2]
    value[:, d:] = jnp.ones((count * rows, d), BF16)
    at_row = lax.broadcasted_iota(jnp.int32, (rows, rows), 0)
    at_key = lax.broadcasted_iota(jnp.int32, (rows, rows), 1)
    allowed = at_key <= at_row
    for i in range(count):
        low, high = i * rows, (i + 1) * rows
        block = query[low:high, :]
        scores = lax.dot_general(block, key[low:high, :], NT, preferred_element_type=F32)
        scores = jnp.where(allowed, scores, -jnp.inf)
        if i:
            left = lax.dot_general(block, key[:low, :], NT, preferred_element_type=F32)
            scores = jnp.concatenate([left, scores], axis=1)
        best = jnp.max(scores, axis=-1, keepdims=True)
        probs = jnp.exp2((scores - best) * scale).astype(BF16)
        summed = jnp.dot(probs, value[:high, :], preferred_element_type=F32)
        result[low:high, :] = (summed[:, :d] / summed[:, d:]).astype(BF16)
    for n in range(hops):
        for f in range(2):
            outs[n][f] = result[places[n][f], :]


def self_attention(chips, same, flipped):
    hops = len(HOPS)
    _, _, rows, width = same[0].shape
    d = HEAD_DIM
    length = 2 * hops * rows
    at = lambda f: pl.BlockSpec((1, 3, rows, d), lambda h: (f, 0, 0, h))
    return pl.pallas_call(
        functools.partial(self_kernel, chips, LOG2E / math.sqrt(d)),
        grid=(width // d,),
        in_specs=[at(0)] * hops + [at(1)] * hops,
        out_specs=[pl.BlockSpec((2, rows, d), lambda h: (0, 0, h))] * hops,
        scratch_shapes=[
            pltpu.VMEM((length, d), BF16),
            pltpu.VMEM((length, d), BF16),
            pltpu.VMEM((length, 2 * d), BF16),
            pltpu.VMEM((length, d), BF16),
        ],
        out_shape=[jax.ShapeDtypeStruct((2, rows, width), BF16)] * hops,
        cost_estimate=cost(7e9, 8e6, length * length),
        compiler_params=params(),
        name="causal",
    )(*same, *flipped)


def unpack_kernel(chips, *refs):
    hops = len(HOPS)
    parts, out = refs[:-1], refs[-1]
    block = parts[0].shape[2]
    reached, _ = partners(chips)
    for n in range(hops):
        for f in range(2):
            columns = pl.ds(pl.multiple_of(reached[n][f] * block, block), block)
            out[:, columns] = parts[f * hops + n][0]


def unpack(chips, same, flipped):
    hops = len(HOPS)
    _, rows, block = same[0].shape
    at = lambda f: pl.BlockSpec((1, rows, block), lambda i: (f, 0, 0))
    shape = (rows, 2 * hops * block)
    return pl.pallas_call(
        functools.partial(unpack_kernel, chips),
        grid=(1,),
        in_specs=[at(0)] * hops + [at(1)] * hops,
        out_specs=pl.BlockSpec(shape, lambda i: (0, 0)),
        out_shape=jax.ShapeDtypeStruct(shape, BF16),
        cost_estimate=cost(0, 4 * math.prod(shape)),
        compiler_params=params(),
        name="unpack",
    )(*same, *flipped)


def requests_of(retrieval_shard, retrieval_row):
    shard_list = retrieval_shard.reshape(-1)
    row_list = retrieval_row.reshape(-1)
    owners = lax.axis_size("db")
    order = jnp.arange(shard_list.shape[0])
    earlier = (order[:, None] > order[None, :]) & (shard_list[:, None] == shard_list[None, :])
    rank = jnp.sum(earlier.astype(jnp.int32), axis=1)
    slot = shard_list * CAP + rank
    hits = jnp.arange(owners * CAP)[:, None] == slot[None, :]
    wanted = jnp.sum(jnp.where(hits, row_list[None, :], 0), axis=1).reshape(owners, CAP)
    return slot, wanted


def shards(
    self_query,
    self_key,
    self_value,
    cross_query,
    retrieval_shard,
    retrieval_row,
    database,
    ffn_in,
    ffn_out,
    cross_projection,
):
    owners = lax.axis_size("db")
    count = lax.axis_size("seq")
    chips = count // 2
    half, deep = ffn_out.shape[0] // 2, ffn_out.shape[1]
    together = lax.optimization_barrier

    part = half_of(ffn_in, ffn_out, cross_projection)
    mine = lax.all_gather(part, "db", axis=0, tiled=True).reshape(owners, -1, deep)

    slot, wanted = requests_of(retrieval_shard, retrieval_row)
    self_query, self_key, self_value, wanted = together((self_query, self_key, self_value, wanted))
    asked = lax.all_to_all(wanted, "db", split_axis=0, concat_axis=0, tiled=True)
    parts = pack(chips, self_query, self_key, self_value)
    same = [parts[0]] + [hop(p, k, 0) for p, k in zip(parts[1:], HOPS[1:])]

    found = fetch(asked, database)
    *same, _ = together((*same, found))
    flipped = [hop(p, 0, 1) for p in same]
    arrived = lax.all_to_all(found, "db", split_axis=0, concat_axis=0, tiled=True)
    ahead = lax.ppermute(cross_query[:STRETCH], "seq", [(i, i - 1) for i in range(1, count)])

    done = self_attention(chips, same, flipped)
    same = [done[0]] + [hop(p, chips - k, 0) for p, k in zip(done[1:], HOPS[1:])]
    flipped = [hop(p, 0, 1) for p in same]
    self_attended = unpack(chips, same, flipped)

    shifted = jnp.concatenate([cross_query[STRETCH - 1 :], ahead[: STRETCH - 1]], axis=0)
    mine, shifted, arrived, _ = together((mine, shifted, arrived, self_attended))
    other = hop(mine, 0, 1)
    total, normed = encode(slot, arrived, mine, half)
    own, sent = cross(total, normed, mine, other, shifted, half)
    before = lax.ppermute(sent, "seq", [(i, i + 1) for i in range(count - 1)])
    cross_attended = mend(own, before)
    return (self_attended, cross_attended)


def solution(mesh):
    in_specs = (
        P(("db", "seq"), None),
        P(("db", "seq"), None),
        P(("db", "seq"), None),
        P(("db", "seq"), None),
        P(("db", "seq"), None),
        P(("db", "seq"), None),
        P("db", None, None),
        P(None, "db"),
        P("db", None),
        P(None, "db"),
    )
    out_specs = (P(("db", "seq"), None), P(("db", "seq"), None))
    return jax.shard_map(shards, mesh=mesh, in_specs=in_specs, out_specs=out_specs, check_vma=False)
```
